32 devices in a mesh: node: 8 (over z, y), local: 4 (over x, core).
Axes of the slice: x: 2, y: 2, z: 4, core: 2. Of those that a mesh axis runs over, the one named last changes fastest.
Arguments:
- tok_x: bfloat16 [64, 2048], P(('node', 'local')), may hold values from -6 to 6
- grad_out: bfloat16 [64, 2048], P(('node', 'local')), may hold values from -6 to 6
- expert_ids: int32 [64, 8], P('node'), may hold values from 0 to 31, as said below
- slot_ids: int32 [64, 8], P('node'), may hold values from 0 to 7, as said below
- route_probs: bfloat16 [64, 8], P('node'), may hold values from 0.099609375 to 1
- gate_weight: bfloat16 [32, 768, 2048], P(('node', 'local')), may hold values from -0.125 to 0.125
- up_weight: bfloat16 [32, 768, 2048], P(('node', 'local')), may hold values from -0.125 to 0.125
- down_weight: bfloat16 [32, 768, 2048], P(('node', 'local')), may hold values from -0.21875 to 0.21875
Outputs:
- grad_x: bfloat16 [64, 2048], P(('node', 'local'))
- grad_probs: float32 [64, 8], P(('node', 'local'))
- grad_gate: float32 [32, 768, 2048], P(('node', 'local'))
- grad_up: float32 [32, 768, 2048], P(('node', 'local'))
- grad_down: float32 [32, 768, 2048], P(('node', 'local'))
The draws below stay inside these ranges and needn't reach their ends.
Inputs may be any that keep to these rules, and one draw needn't show every extreme that they name: `expert_ids`: each token names 8 different experts. Among the 8 tokens of every index of node, some expert is named by all 8 tokens. `slot_ids`: the pairs of the 8 tokens of one index of node that name one expert carry the slots 0, 1, 2 and so on, each once.
All inputs are finite; a program needn't handle non-finite values.
Results may differ from the reference program's by a relative error of at most 0.0049.
Values may be sent and summed in bfloat16 or wider, within the bound.
A program may use at most 64 MiB of HBM per device.

```python
import math
import jax
import jax.numpy as jnp
from jax import lax

D = 2048
FF = 768
TOPK = 8
EXPERTS = 32
OWN = 1
HID_DEV = 768
NODE_TOK = 8
TOKENS = 64
CAPN = 7
CAPE = 56


def slot_ranks(items):
    order_keys, experts_row = items
    same_expert = experts_row[None, :] == experts_row[:, None]
    earlier = order_keys[None, :] < order_keys[:, None]
    return jnp.sum((same_expert & earlier).astype(jnp.int32), axis=1).astype(jnp.int32)


def routing_table(key):
    base = jax.random.fold_in(key, 11)
    key_score = jax.random.fold_in(base, 0)
    key_favour = jax.random.fold_in(base, 1)
    key_hot = jax.random.fold_in(base, 2)
    key_order = jax.random.fold_in(base, 4)
    groups = TOKENS // NODE_TOK
    scores = jax.random.randint(key_score, (groups, NODE_TOK, EXPERTS), 0, 1 << 20)
    favour = jax.random.randint(key_favour, (groups, 1, EXPERTS), 0, 1 << 19)
    scores = scores + favour
    hottest = jax.random.randint(key_hot, (groups, 1, 1), 0, EXPERTS)
    forced = jnp.arange(EXPERTS, dtype=jnp.int32)[None, None, :] == hottest
    forced = jnp.broadcast_to(forced, (groups, NODE_TOK, EXPERTS))
    scores = jnp.where(forced, 1 << 21, scores)
    distinct = scores * EXPERTS + jnp.arange(EXPERTS, dtype=jnp.int32)[None, None, :]
    unused, chosen = lax.top_k(distinct, TOPK)
    chosen = chosen.astype(jnp.int32)
    pair_total = NODE_TOK * TOPK
    order_keys = jax.random.randint(key_order, (groups, pair_total), 0, 1 << 16) * pair_total + jnp.arange(pair_total, dtype=jnp.int32)[None, :]
    slots = lax.map(slot_ranks, (order_keys, chosen.reshape(groups, pair_total)))
    return (chosen.reshape(TOKENS, TOPK), slots.reshape(TOKENS, TOPK).astype(jnp.int32))


def draw_expert_ids(key, part):
    experts_all, slots_all = routing_table(key)
    return experts_all


def draw_slot_ids(key, part):
    experts_all, slots_all = routing_table(key)
    return slots_all


def level_of(key, extent, shards, low, high):
    level, own = 1.0, jax.random.fold_in(key, 6)
    for axis_at, shards_of in shards:
        steps = jnp.exp(jax.random.uniform(jax.random.fold_in(own, axis_at), (shards_of,), jnp.float32, low / len(shards), high / len(shards)))
        level = level * jnp.repeat(steps, extent[axis_at] // shards_of).reshape([-1 if axis == axis_at else 1 for axis in range(len(extent))])
    return level


def bell_draw(own_key, dims, scale, limit, cuts=(), kind=jnp.bfloat16):
    drawn = jax.random.normal(own_key, dims, jnp.float32) * scale
    if len(cuts) > 0:
        drawn = level_of(own_key, dims, cuts, -0.22, 0.18) * drawn
    return jnp.clip(drawn, min=-limit, max=limit).astype(kind)


def setup_inputs(seed: int = 0) -> dict:
    arg_keys = jax.random.split(jax.random.key(seed), 9)
    return {
        "tok_x": bell_draw(arg_keys[0], (TOKENS, D), 1.0, 6.0, ((0, 32),)),
        "grad_out": bell_draw(arg_keys[1], (TOKENS, D), 1.0, 6.0, ((0, 32),)),
        "expert_ids": draw_expert_ids(jax.random.fold_in(arg_keys[8], 71), 0),
        "slot_ids": draw_slot_ids(jax.random.fold_in(arg_keys[8], 71), 0),
        "route_probs": jnp.clip(jnp.exp(math.log(1.0) - 2.306499 * jax.random.uniform(arg_keys[4], (TOKENS, TOPK), jnp.float32) ** level_of(arg_keys[4], (TOKENS, TOPK), ((0, 8),), -0.2, 0.2)), 0.099609375, 1.0).astype(jnp.bfloat16),
        "gate_weight": bell_draw(arg_keys[5], (EXPERTS * OWN, HID_DEV, D), D ** -0.5, 0.125, ((0, 32),)),
        "up_weight": bell_draw(arg_keys[6], (EXPERTS * OWN, HID_DEV, D), D ** -0.5, 0.125, ((0, 32),)),
        "down_weight": bell_draw(arg_keys[7], (EXPERTS * OWN, HID_DEV, D), FF ** -0.5, 0.21875, ((0, 32),)),
    }


def expert_grads(rows_x, rows_d, rows_p, w_gate_e, w_up_e, w_down_e):
    gate_pre = jnp.dot(rows_x, w_gate_e.T, preferred_element_type=jnp.float32)
    up_pre = jnp.dot(rows_x, w_up_e.T, preferred_element_type=jnp.float32)
    sigmoid_gate = jax.nn.sigmoid(gate_pre)
    activated = gate_pre * sigmoid_gate
    hidden = activated * up_pre
    back_proj = jnp.dot(rows_d, w_down_e.T, preferred_element_type=jnp.float32)
    pair_grad = jnp.sum(hidden * back_proj, axis=1)
    d_hidden = rows_p[:, None] * back_proj
    d_gate = (d_hidden * up_pre * sigmoid_gate * (1.0 + gate_pre * (1.0 - sigmoid_gate))).astype(jnp.bfloat16)
    d_up = (d_hidden * activated).astype(jnp.bfloat16)
    scaled_hidden = (rows_p[:, None] * hidden).astype(jnp.bfloat16)
    input_grad = jnp.dot(d_gate, w_gate_e, preferred_element_type=jnp.float32) + jnp.dot(d_up, w_up_e, preferred_element_type=jnp.float32)
    gate_grad = jnp.dot(d_gate.T, rows_x, preferred_element_type=jnp.float32)
    up_grad = jnp.dot(d_up.T, rows_x, preferred_element_type=jnp.float32)
    down_grad = jnp.dot(scaled_hidden.T, rows_d, preferred_element_type=jnp.float32)
    return input_grad, pair_grad, gate_grad, up_grad, down_grad


def reference(tok_x, grad_out, expert_ids, slot_ids, route_probs, gate_weight, up_weight, down_weight):
    pair_count = TOKENS * TOPK
    flat_expert = expert_ids.reshape(-1).astype(jnp.int32)
    flat_slot = slot_ids.reshape(-1).astype(jnp.int32)
    pair_ids = jnp.arange(pair_count, dtype=jnp.int32)
    group_ids = (pair_ids // (TOPK * NODE_TOK)).astype(jnp.int32)
    is_kept = flat_slot < CAPN
    target = jnp.where(is_kept, flat_expert * CAPE + group_ids * CAPN + flat_slot, EXPERTS * CAPE).astype(jnp.int32)
    slot_table = jnp.full((EXPERTS * CAPE,), pair_count, dtype=jnp.int32).at[target].set(pair_ids, mode="drop")
    slot_table = slot_table.reshape(EXPERTS, CAPE)
    flat_probs = route_probs.reshape(-1).astype(jnp.float32)
    gate_all = gate_weight.reshape(EXPERTS, FF, D)
    up_all = up_weight.reshape(EXPERTS, FF, D)
    down_all = down_weight.reshape(EXPERTS, FF, D)

    def one_expert(items):
        table_row, w_gate_e, w_up_e, w_down_e = items
        token_rows = (table_row // TOPK).astype(jnp.int32)
        rows_x = jnp.take(tok_x, token_rows, axis=0, mode="fill", fill_value=0)
        rows_d = jnp.take(grad_out, token_rows, axis=0, mode="fill", fill_value=0)
        rows_p = jnp.take(flat_probs, table_row, mode="fill", fill_value=0)
        return expert_grads(rows_x, rows_d, rows_p, w_gate_e, w_up_e, w_down_e)

    input_grad, pair_grad, gate_grad, up_grad, down_grad = lax.map(one_expert, (slot_table, gate_all, up_all, down_all))
    all_rows = (slot_table // TOPK).reshape(-1).astype(jnp.int32)
    grad_x = jnp.zeros((TOKENS, D), jnp.float32).at[all_rows].add(input_grad.reshape(-1, D), mode="drop")
    grad_probs = jnp.zeros((pair_count,), jnp.float32).at[slot_table.reshape(-1)].add(pair_grad.reshape(-1), mode="drop")
    return (grad_x.astype(jnp.bfloat16), grad_probs.reshape(TOKENS, TOPK), gate_grad.reshape(EXPERTS * OWN, HID_DEV, D), up_grad.reshape(EXPERTS * OWN, HID_DEV, D), down_grad.reshape(EXPERTS * OWN, HID_DEV, D))
```

```python
import functools

import jax
import jax.numpy as jnp
from jax import lax
from jax.experimental import pallas as pl
from jax.experimental.pallas import tpu as pltpu
from jax.sharding import PartitionSpec as P

EXP_NODE = 4
CAPN = 7
MESH = pl.DeviceIdType.MESH


contract_last = (((1,), (1,)), ((), ()))
contract_first = (((0,), (0,)), ((), ()))


def owner_grads(owner_x, owner_d, owner_p, w_gate_rows, w_up_rows, w_down_rows):
    gate_pre = lax.dot_general(
        owner_x, w_gate_rows, contract_last, preferred_element_type=jnp.float32
    )
    up_pre = lax.dot_general(owner_x, w_up_rows, contract_last, preferred_element_type=jnp.float32)
    sigmoid_gate = jax.nn.sigmoid(gate_pre)
    activated = gate_pre * sigmoid_gate
    hidden = activated * up_pre
    back_proj = lax.dot_general(
        owner_d, w_down_rows, contract_last, preferred_element_type=jnp.float32
    )
    pair_grad = jnp.sum(hidden * back_proj, axis=1)
    d_hidden = owner_p[:, None] * back_proj
    d_gate = (d_hidden * up_pre * sigmoid_gate * (1.0 + gate_pre * (1.0 - sigmoid_gate))).astype(
        jnp.bfloat16
    )
    d_up = (d_hidden * activated).astype(jnp.bfloat16)
    scaled_hidden = (owner_p[:, None] * hidden).astype(jnp.bfloat16)
    input_grad = jnp.dot(d_gate, w_gate_rows, preferred_element_type=jnp.float32) + jnp.dot(
        d_up, w_up_rows, preferred_element_type=jnp.float32
    )
    gate_grad = lax.dot_general(d_gate, owner_x, contract_first, preferred_element_type=jnp.float32)
    up_grad = lax.dot_general(d_up, owner_x, contract_first, preferred_element_type=jnp.float32)
    down_grad = lax.dot_general(
        scaled_hidden, owner_d, contract_first, preferred_element_type=jnp.float32
    )
    return (input_grad, pair_grad, gate_grad, up_grad, down_grad)


def local(tok_x, grad_out, expert_ids, slot_ids, route_probs, gate_weight, up_weight, down_weight):
    node_count = lax.axis_size("node")
    owners = lax.axis_size("local") // EXP_NODE
    place = lax.axis_index("local")
    own_class = place // owners
    node_tokens = expert_ids.shape[0]
    top_count = expert_ids.shape[1]
    model_width = tok_x.shape[1]
    pair_count = node_tokens * top_count
    node_x, node_d = (
        lax.all_gather(tok_x, "local", axis=0, tiled=True),
        lax.all_gather(grad_out, "local", axis=0, tiled=True),
    )
    flat_expert = expert_ids.reshape(-1)
    flat_slot = slot_ids.reshape(-1)
    pair_ids = jnp.arange(pair_count, dtype=jnp.int32)
    is_mine = (flat_expert % EXP_NODE == own_class) & (flat_slot < CAPN)
    target = jnp.where(is_mine, flat_expert // EXP_NODE * CAPN + flat_slot, node_count * CAPN)
    slot_table = (
        jnp.full((node_count * CAPN,), pair_count, jnp.int32).at[target].set(pair_ids, mode="drop")
    )
    token_rows = slot_table // top_count
    outbox_p = jnp.take(route_probs.reshape(-1), slot_table, mode="fill", fill_value=0).reshape(
        node_count, CAPN
    )
    outbox_x = jnp.take(node_x, token_rows, axis=0, mode="fill", fill_value=0).reshape(
        node_count, CAPN, model_width
    )
    outbox_d = jnp.take(node_d, token_rows, axis=0, mode="fill", fill_value=0).reshape(
        node_count, CAPN, model_width
    )
    arrived_x, arrived_d, arrived_p = (
        lax.all_to_all(outbox_x, "node", split_axis=0, concat_axis=0, tiled=True),
        lax.all_to_all(outbox_d, "node", split_axis=0, concat_axis=0, tiled=True),
        lax.all_to_all(outbox_p, "node", split_axis=0, concat_axis=0, tiled=True),
    )
    owner_x = arrived_x.reshape(-1, model_width)
    owner_d = arrived_d.reshape(-1, model_width)
    owner_p = arrived_p.reshape(-1).astype(jnp.float32)
    input_grad, pair_grad, gate_grad, up_grad, down_grad = owner_grads(
        owner_x, owner_d, owner_p, gate_weight[0], up_weight[0], down_weight[0]
    )
    token_hits = (token_rows[None, :] == jnp.arange(node_tokens, dtype=jnp.int32)[:, None]).astype(
        jnp.float32
    )
    back_x, back_p = (
        lax.all_to_all(
            input_grad.reshape(node_count, CAPN, model_width),
            "node",
            split_axis=0,
            concat_axis=0,
            tiled=True,
        ),
        lax.all_to_all(
            pair_grad.reshape(node_count, CAPN), "node", split_axis=0, concat_axis=0, tiled=True
        ),
    )
    token_x = jnp.dot(
        token_hits,
        back_x.reshape(-1, model_width),
        precision=lax.Precision.HIGHEST,
        preferred_element_type=jnp.float32,
    )
    token_p = (
        jnp.zeros((pair_count,), jnp.float32)
        .at[slot_table]
        .add(back_p.reshape(-1), mode="drop")
        .reshape(node_tokens, top_count)
    )
    summed_x, summed_p = (
        lax.psum_scatter(token_x, "local", scatter_dimension=0, tiled=True),
        lax.psum_scatter(token_p, "local", scatter_dimension=0, tiled=True),
    )
    return (
        summed_x.astype(jnp.bfloat16),
        summed_p,
        gate_grad[None],
        up_grad[None],
        down_grad[None],
    )


LANES = 128
PIECE = 16
DENSE_TOKENS = 64


def one_hot_rows(source, width):
    columns = lax.broadcasted_iota(jnp.int32, (source.shape[0], width), 1)
    return jnp.where(columns == source, 1.0, 0.0).astype(jnp.bfloat16)


def exchange_kernel(
    node_count,
    local_count,
    tok_ref,
    grad_ref,
    ids_ref,
    slots_ref,
    probs_ref,
    gate_hbm,
    up_hbm,
    down_hbm,
    x_ref,
    d_ref,
    dgate_ref,
    dup_ref,
    scaled_ref,
    gx_ref,
    gp_ref,
    gate_w,
    up_w,
    down_w,
    pieces,
    order,
    total,
    out_local,
    in_local,
    out_node,
    in_node,
    weight_sem,
    send_sem,
    piece_sem,
    local_send_sem,
    local_recv_sem,
    node_send_sem,
    node_recv_sem,
):
    f32, bf16 = jnp.float32, jnp.bfloat16
    node, place = lax.axis_index("node"), lax.axis_index("local")
    experts = node_count * EXP_NODE
    expert = node * local_count + place
    own, width = tok_ref.shape
    tokens = node_count * local_count * own
    chunks, chunk = gate_w.shape[0], gate_w.shape[1]
    quarters = PIECE // (2 * own)
    span = width // quarters
    eighths = PIECE // own
    fine = width // eighths

    loads = []
    for c in range(chunks):
        for w, (source, target) in enumerate(
            ((gate_hbm, gate_w), (up_hbm, up_w), (down_hbm, down_w))
        ):
            copy = pltpu.make_async_copy(
                source.at[0, pl.ds(c * chunk, chunk), :], target.at[c], weight_sem.at[w, c]
            )
            copy.start()
            loads.append(copy)

    barrier = pltpu.get_barrier_semaphore()
    for step in range(1, node_count):
        pl.semaphore_signal(
            barrier,
            inc=1,
            device_id=(lax.rem(node + step, node_count), place),
            device_id_type=MESH,
        )
    for step in range(1, local_count):
        pl.semaphore_signal(
            barrier,
            inc=1,
            device_id=(node, lax.rem(place + step, local_count)),
            device_id_type=MESH,
        )

    kept_ids = jnp.where(slots_ref[...] < CAPN, ids_ref[...], -1)
    probs = probs_ref[...].astype(f32)
    node_tokens, top = kept_ids.shape
    lane = lax.broadcasted_iota(jnp.int32, (node_tokens, LANES), 1)
    dense = jnp.zeros((node_tokens, LANES), f32)
    for k in range(top):
        dense = dense + jnp.where(lane == kept_ids[:, k : k + 1], probs[:, k : k + 1], 0.0)
    token_row = lax.broadcasted_iota(jnp.int32, (node_tokens, LANES), 0)
    row = lax.broadcasted_iota(jnp.int32, (PIECE, span), 0)
    row_p = lax.broadcasted_iota(jnp.int32, (PIECE, LANES), 0)
    packed = jnp.zeros((PIECE, span), f32)
    packed_p = jnp.zeros((PIECE, LANES), f32)
    for which, source in enumerate((tok_ref, grad_ref)):
        rows = source[...].astype(f32)
        for t in range(own):
            for q in range(quarters):
                packed = jnp.where(
                    row == (which * own + t) * quarters + q,
                    rows[t : t + 1, q * span : (q + 1) * span],
                    packed,
                )
    for t in range(own):
        line = jnp.sum(jnp.where(token_row == place * own + t, dense, 0.0), axis=0, keepdims=True)
        packed_p = jnp.where(row_p == t * quarters, line, packed_p)
    me = node * local_count + place
    pieces[me, :, :span] = packed.astype(bf16)
    pieces[me, :, span:] = packed_p.astype(bf16)

    pl.semaphore_wait(barrier, node_count + local_count - 2)

    sent = []

    def send_piece(piece, target):
        copy = pltpu.make_async_remote_copy(
            src_ref=pieces.at[piece],
            dst_ref=pieces.at[piece],
            send_sem=send_sem.at[len(sent)],
            recv_sem=piece_sem.at[piece],
            device_id=target,
            device_id_type=MESH,
        )
        copy.start()
        sent.append(copy)

    def await_piece(piece):
        pltpu.make_async_remote_copy(
            src_ref=pieces.at[piece],
            dst_ref=pieces.at[piece],
            send_sem=send_sem.at[0],
            recv_sem=piece_sem.at[piece],
            device_id=(node, place),
            device_id_type=MESH,
        ).wait_recv()

    chips = local_count // 2
    chip, core = place // 2, lax.rem(place, 2)
    mate = (node, chip * 2 + 1 - core)
    for step in range(1, node_count):
        send_piece(me, (lax.rem(node + step, node_count), place))
    for step in range(1, chips):
        send_piece(me, (node, lax.rem(chip + step, chips) * 2 + core))
    send_piece(me, mate)

    i = lax.broadcasted_iota(jnp.int32, (order.shape[0], LANES), 0)
    which, q, tok = i // (quarters * tokens), (i // tokens) % quarters, i % tokens
    l, n, t = tok // (own * node_count), (tok // own) % node_count, tok % own
    source = (n * local_count + l) * PIECE + (which * own + t) * quarters + q
    for block in range(order.shape[1] // LANES):
        columns = lax.broadcasted_iota(jnp.int32, (order.shape[0], LANES), 1) + block * LANES
        order[:, block * LANES : (block + 1) * LANES] = jnp.where(
            columns == source, 1.0, 0.0
        ).astype(bf16)

    for step in range(1, node_count):
        piece = lax.rem(node + node_count - step, node_count) * local_count + place
        await_piece(piece)
        for hop in range(1, chips):
            send_piece(piece, (node, lax.rem(chip + hop, chips) * 2 + core))
        send_piece(piece, mate)
    for step in range(node_count):
        for hop in range(1, chips):
            piece = (
                lax.rem(node + node_count - step, node_count) * local_count
                + lax.rem(chip + chips - hop, chips) * 2
                + core
            )
            await_piece(piece)
            send_piece(piece, mate)
    for step in range(node_count):
        for hop in range(chips):
            piece = (
                lax.rem(node + node_count - step, node_count) * local_count
                + lax.rem(chip + chips - hop, chips) * 2
                + 1
                - core
            )
            await_piece(piece)

    gathered = pieces[...].reshape(order.shape[0], span + LANES)
    for half in range(2):
        columns = span // 2
        at = half * columns
        sorted_rows = jnp.dot(
            order[...], gathered[:, at : at + columns], preferred_element_type=f32
        ).astype(bf16)
        for which, target in enumerate((x_ref, d_ref)):
            for q in range(quarters):
                first = (which * quarters + q) * tokens
                target[:, q * span + at : q * span + at + columns] = sorted_rows[
                    first : first + tokens
                ]
    weights = jnp.dot(order[:tokens, :], gathered[:, span:], preferred_element_type=f32)
    lane = lax.broadcasted_iota(jnp.int32, (tokens, LANES), 1)
    p_col = jnp.sum(jnp.where(lane == expert, weights, 0.0), axis=1, keepdims=True)

    contract_last = (((1,), (1,)), ((), ()))
    pair = jnp.zeros((tokens, 1), f32)
    for c in range(chunks):
        for copy in loads[3 * c : 3 * c + 3]:
            copy.wait()
        gate_pre = lax.dot_general(
            x_ref[...], gate_w[c], contract_last, preferred_element_type=f32
        )
        up_pre = lax.dot_general(x_ref[...], up_w[c], contract_last, preferred_element_type=f32)
        back = lax.dot_general(d_ref[...], down_w[c], contract_last, preferred_element_type=f32)
        s = jax.nn.sigmoid(gate_pre)
        activated = gate_pre * s
        hidden = activated * up_pre
        pair = pair + jnp.sum(hidden * back, axis=1, keepdims=True)
        d_hidden = p_col * back
        d_gate = (d_hidden * up_pre * s * (1.0 + gate_pre * (1.0 - s))).astype(bf16)
        d_up = (d_hidden * activated).astype(bf16)
        at = pl.ds(c * chunk, chunk)
        dgate_ref[:, at] = d_gate
        dup_ref[:, at] = d_up
        scaled_ref[:, at] = (p_col * hidden).astype(bf16)
        for half in range(4):
            columns = pl.ds(half * (width // 4), width // 4)
            part = jnp.dot(d_gate, gate_w[c, :, columns], preferred_element_type=f32) + jnp.dot(
                d_up, up_w[c, :, columns], preferred_element_type=f32
            )
            if c == 0:
                total[:, columns] = part
            else:
                total[:, columns] += part

    high = pair.astype(bf16).astype(f32)
    total[:, width:] = jnp.where(
        lane == expert, high, jnp.where(lane == expert + experts, pair - high, 0.0)
    )
    out_local[...] = total[...].astype(bf16).reshape(out_local.shape)
    group = own * node_count
    copies = []
    for step in range(1, local_count):
        peer = lax.rem(place + step, local_count)
        copy = pltpu.make_async_remote_copy(
            src_ref=out_local.at[peer],
            dst_ref=in_local.at[place],
            send_sem=local_send_sem.at[step],
            recv_sem=local_recv_sem.at[place],
            device_id=(node, peer),
            device_id_type=MESH,
        )
        copy.start()
        copies.append(copy)
    summed = total[pl.ds(pl.multiple_of(place * group, group), group), :]
    for step in range(1, local_count):
        peer = lax.rem(place + local_count - step, local_count)
        pltpu.make_async_remote_copy(
            src_ref=out_local.at[peer],
            dst_ref=in_local.at[peer],
            send_sem=local_send_sem.at[0],
            recv_sem=local_recv_sem.at[peer],
            device_id=(node, peer),
            device_id_type=MESH,
        ).wait_recv()
        summed = summed + in_local[peer].astype(f32)

    summed = summed.astype(bf16)
    count = eighths * group
    stacked = jnp.concatenate(
        [summed[:, e * fine : (e + 1) * fine] for e in range(eighths)], axis=0
    )
    i = lax.broadcasted_iota(jnp.int32, (count, 1), 0)
    n, t, e = i // PIECE, (i // eighths) % own, i % eighths
    spread = one_hot_rows(e * group + n * own + t, count)
    out_node[:, :, :fine] = (
        jnp.dot(spread, stacked, preferred_element_type=f32)
        .astype(bf16)
        .reshape(node_count, PIECE, fine)
    )
    tail = jnp.where(e == 0, n * own + t, -1)
    out_node[:, :, fine:] = (
        jnp.dot(one_hot_rows(tail, group), summed[:, width:], preferred_element_type=f32)
        .astype(bf16)
        .reshape(node_count, PIECE, LANES)
    )
    for step in range(1, node_count):
        peer = lax.rem(node + step, node_count)
        copy = pltpu.make_async_remote_copy(
            src_ref=out_node.at[peer],
            dst_ref=in_node.at[node],
            send_sem=node_send_sem.at[step],
            recv_sem=node_recv_sem.at[node],
            device_id=(peer, place),
            device_id_type=MESH,
        )
        copy.start()
        copies.append(copy)
    result = out_node[node].astype(f32)
    for step in range(1, node_count):
        peer = lax.rem(node + node_count - step, node_count)
        pltpu.make_async_remote_copy(
            src_ref=out_node.at[peer],
            dst_ref=in_node.at[peer],
            send_sem=node_send_sem.at[0],
            recv_sem=node_recv_sem.at[peer],
            device_id=(peer, place),
            device_id_type=MESH,
        ).wait_recv()
        result = result + in_node[peer].astype(f32)

    rounded = result[:, :fine].astype(bf16)
    t8 = lax.broadcasted_iota(jnp.int32, (8, 1), 0)
    for e in range(eighths):
        picked = jnp.dot(
            one_hot_rows(t8 * eighths + e, PIECE), rounded, preferred_element_type=f32
        )
        gx_ref[:, e * fine : (e + 1) * fine] = picked[:own].astype(bf16)
    row = lax.broadcasted_iota(jnp.int32, (PIECE, LANES), 0)
    token_row = lax.broadcasted_iota(jnp.int32, (node_tokens, top), 0)
    eye = lax.broadcasted_iota(jnp.int32, (top, top), 0) == lax.broadcasted_iota(
        jnp.int32, (top, top), 1
    )
    lane = lax.broadcasted_iota(jnp.int32, (top, LANES), 1).astype(f32)
    ids_f = kept_ids.astype(f32)
    for t in range(own):
        line = jnp.sum(jnp.where(row == t * eighths, result[:, fine:], 0.0), axis=0, keepdims=True)
        ids_row = jnp.sum(
            jnp.where(token_row == place * own + t, ids_f, 0.0), axis=0, keepdims=True
        )
        ids_col = jnp.sum(jnp.where(eye, ids_row, 0.0), axis=1, keepdims=True)
        hit = (ids_col >= 0.0) & ((lane == ids_col) | (lane == ids_col + experts))
        found = jnp.sum(jnp.where(hit, line, 0.0), axis=1, keepdims=True)
        gp_ref[t : t + 1, :] = jnp.sum(jnp.where(eye, found, 0.0), axis=0, keepdims=True)

    for copy in sent:
        copy.wait_send()
    for copy in copies:
        copy.wait_send()


def outer_kernel(x_ref, d_ref, dgate_ref, dup_ref, scaled_ref, gate_ref, up_ref, down_ref):
    contract_first = (((0,), (0,)), ((), ()))
    for left, right, target in (
        (dgate_ref, x_ref, gate_ref),
        (dup_ref, x_ref, up_ref),
        (scaled_ref, d_ref, down_ref),
    ):
        target[0] = lax.dot_general(
            left[...], right[...], contract_first, preferred_element_type=jnp.float32
        )


def dense_local(
    tok_x, grad_out, expert_ids, slot_ids, route_probs, gate_weight, up_weight, down_weight
):
    node_count, local_count = lax.axis_size("node"), lax.axis_size("local")
    own, width = tok_x.shape
    top = expert_ids.shape[1]
    hidden = gate_weight.shape[1]
    devices = node_count * local_count
    tokens = devices * own
    chunk = 256 if hidden % 256 == 0 else hidden
    chunks = hidden // chunk
    quarters = PIECE // (2 * own)
    span = width // quarters
    fine = width * own // PIECE
    f32, bf16 = jnp.float32, jnp.bfloat16
    vmem = pl.BlockSpec(memory_space=pltpu.VMEM)
    hbm = pl.BlockSpec(memory_space=pl.ANY)
    dma = pltpu.SemaphoreType.DMA
    group = own * node_count
    rows_x, rows_d, d_gate, d_up, scaled, grad_x, grad_probs = pl.pallas_call(
        functools.partial(exchange_kernel, node_count, local_count),
        out_shape=(
            jax.ShapeDtypeStruct((tokens, width), bf16),
            jax.ShapeDtypeStruct((tokens, width), bf16),
            jax.ShapeDtypeStruct((tokens, hidden), bf16),
            jax.ShapeDtypeStruct((tokens, hidden), bf16),
            jax.ShapeDtypeStruct((tokens, hidden), bf16),
            jax.ShapeDtypeStruct((own, width), bf16),
            jax.ShapeDtypeStruct((own, top), f32),
        ),
        in_specs=[vmem] * 5 + [hbm] * 3,
        out_specs=(vmem,) * 7,
        scratch_shapes=[
            pltpu.VMEM((chunks, chunk, width), bf16),
            pltpu.VMEM((chunks, chunk, width), bf16),
            pltpu.VMEM((chunks, chunk, width), bf16),
            pltpu.VMEM((devices, PIECE, span + LANES), bf16),
            pltpu.VMEM((devices * PIECE, devices * PIECE), bf16),
            pltpu.VMEM((tokens, width + LANES), f32),
            pltpu.VMEM((local_count, group, width + LANES), bf16),
            pltpu.VMEM((local_count, group, width + LANES), bf16),
            pltpu.VMEM((node_count, PIECE, fine + LANES), bf16),
            pltpu.VMEM((node_count, PIECE, fine + LANES), bf16),
            dma((3, chunks)),
            dma((devices,)),
            dma((devices,)),
            dma((local_count,)),
            dma((local_count,)),
            dma((node_count,)),
            dma((node_count,)),
        ],
        compiler_params=pltpu.CompilerParams(
            collective_id=0, has_side_effects=True, vmem_limit_bytes=48 * 1024 * 1024
        ),
    )(tok_x, grad_out, expert_ids, slot_ids, route_probs, gate_weight, up_weight, down_weight)
    block = 128 if hidden % 128 == 0 else hidden
    grad = jax.ShapeDtypeStruct((1, hidden, width), f32)
    whole = pl.BlockSpec((tokens, width), lambda i: (0, 0))
    part = pl.BlockSpec((tokens, block), lambda i: (0, i))
    out = pl.BlockSpec((1, block, width), lambda i: (0, i, 0))
    gate_grad, up_grad, down_grad = pl.pallas_call(
        outer_kernel,
        out_shape=(grad, grad, grad),
        grid=(hidden // block,),
        in_specs=[whole, whole, part, part, part],
        out_specs=(out, out, out),
        compiler_params=pltpu.CompilerParams(vmem_limit_bytes=32 * 1024 * 1024),
    )(rows_x, rows_d, d_gate, d_up, scaled)
    return grad_x, grad_probs, gate_grad, up_grad, down_grad


def solution(mesh):
    in_specs = (
        P(("node", "local"), None),
        P(("node", "local"), None),
        P("node", None),
        P("node", None),
        P("node", None),
        P(("node", "local"), None, None),
        P(("node", "local"), None, None),
        P(("node", "local"), None, None),
    )
    out_specs = (
        P(("node", "local"), None),
        P(("node", "local"), None),
        P(("node", "local"), None, None),
        P(("node", "local"), None, None),
        P(("node", "local"), None, None),
    )
    node_count, local_count = mesh.shape["node"], mesh.shape["local"]

    def step(*args):
        tokens = args[0].shape[0] * node_count * local_count
        dense = (
            tokens <= DENSE_TOKENS
            and local_count == EXP_NODE
            and 2 * EXP_NODE * node_count <= LANES
        )
        return (dense_local if dense else local)(*args)

    return jax.shard_map(step, mesh=mesh, in_specs=in_specs, out_specs=out_specs, check_vma=False)
```

```python
import functools

import jax
import jax.numpy as jnp
from jax import lax
from jax.experimental import pallas as pl
from jax.experimental.pallas import tpu as pltpu
from jax.sharding import PartitionSpec as P

EXP_NODE = 4
CAPN = 7
MESH = pl.DeviceIdType.MESH


contract_last = (((1,), (1,)), ((), ()))
contract_first = (((0,), (0,)), ((), ()))


def owner_grads(owner_x, owner_d, owner_p, w_gate_rows, w_up_rows, w_down_rows):
    gate_pre = lax.dot_general(
        owner_x, w_gate_rows, contract_last, preferred_element_type=jnp.float32
    )
    up_pre = lax.dot_general(owner_x, w_up_rows, contract_last, preferred_element_type=jnp.float32)
    sigmoid_gate = jax.nn.sigmoid(gate_pre)
    activated = gate_pre * sigmoid_gate
    hidden = activated * up_pre
    back_proj = lax.dot_general(
        owner_d, w_down_rows, contract_last, preferred_element_type=jnp.float32
    )
    pair_grad = jnp.sum(hidden * back_proj, axis=1)
    d_hidden = owner_p[:, None] * back_proj
    d_gate = (d_hidden * up_pre * sigmoid_gate * (1.0 + gate_pre * (1.0 - sigmoid_gate))).astype(
        jnp.bfloat16
    )
    d_up = (d_hidden * activated).astype(jnp.bfloat16)
    scaled_hidden = (owner_p[:, None] * hidden).astype(jnp.bfloat16)
    input_grad = jnp.dot(d_gate, w_gate_rows, preferred_element_type=jnp.float32) + jnp.dot(
        d_up, w_up_rows, preferred_element_type=jnp.float32
    )
    gate_grad = lax.dot_general(d_gate, owner_x, contract_first, preferred_element_type=jnp.float32)
    up_grad = lax.dot_general(d_up, owner_x, contract_first, preferred_element_type=jnp.float32)
    down_grad = lax.dot_general(
        scaled_hidden, owner_d, contract_first, preferred_element_type=jnp.float32
    )
    return (input_grad, pair_grad, gate_grad, up_grad, down_grad)


def local(tok_x, grad_out, expert_ids, slot_ids, route_probs, gate_weight, up_weight, down_weight):
    node_count = lax.axis_size("node")
    owners = lax.axis_size("local") // EXP_NODE
    place = lax.axis_index("local")
    own_class = place // owners
    node_tokens = expert_ids.shape[0]
    top_count = expert_ids.shape[1]
    model_width = tok_x.shape[1]
    pair_count = node_tokens * top_count
    node_x, node_d = (
        lax.all_gather(tok_x, "local", axis=0, tiled=True),
        lax.all_gather(grad_out, "local", axis=0, tiled=True),
    )
    flat_expert = expert_ids.reshape(-1)
    flat_slot = slot_ids.reshape(-1)
    pair_ids = jnp.arange(pair_count, dtype=jnp.int32)
    is_mine = (flat_expert % EXP_NODE == own_class) & (flat_slot < CAPN)
    target = jnp.where(is_mine, flat_expert // EXP_NODE * CAPN + flat_slot, node_count * CAPN)
    slot_table = (
        jnp.full((node_count * CAPN,), pair_count, jnp.int32).at[target].set(pair_ids, mode="drop")
    )
    token_rows = slot_table // top_count
    outbox_p = jnp.take(route_probs.reshape(-1), slot_table, mode="fill", fill_value=0).reshape(
        node_count, CAPN
    )
    outbox_x = jnp.take(node_x, token_rows, axis=0, mode="fill", fill_value=0).reshape(
        node_count, CAPN, model_width
    )
    outbox_d = jnp.take(node_d, token_rows, axis=0, mode="fill", fill_value=0).reshape(
        node_count, CAPN, model_width
    )
    arrived_x, arrived_d, arrived_p = (
        lax.all_to_all(outbox_x, "node", split_axis=0, concat_axis=0, tiled=True),
        lax.all_to_all(outbox_d, "node", split_axis=0, concat_axis=0, tiled=True),
        lax.all_to_all(outbox_p, "node", split_axis=0, concat_axis=0, tiled=True),
    )
    owner_x = arrived_x.reshape(-1, model_width)
    owner_d = arrived_d.reshape(-1, model_width)
    owner_p = arrived_p.reshape(-1).astype(jnp.float32)
    input_grad, pair_grad, gate_grad, up_grad, down_grad = owner_grads(
        owner_x, owner_d, owner_p, gate_weight[0], up_weight[0], down_weight[0]
    )
    token_hits = (token_rows[None, :] == jnp.arange(node_tokens, dtype=jnp.int32)[:, None]).astype(
        jnp.float32
    )
    back_x, back_p = (
        lax.all_to_all(
            input_grad.reshape(node_count, CAPN, model_width),
            "node",
            split_axis=0,
            concat_axis=0,
            tiled=True,
        ),
        lax.all_to_all(
            pair_grad.reshape(node_count, CAPN), "node", split_axis=0, concat_axis=0, tiled=True
        ),
    )
    token_x = jnp.dot(
        token_hits,
        back_x.reshape(-1, model_width),
        precision=lax.Precision.HIGHEST,
        preferred_element_type=jnp.float32,
    )
    token_p = (
        jnp.zeros((pair_count,), jnp.float32)
        .at[slot_table]
        .add(back_p.reshape(-1), mode="drop")
        .reshape(node_tokens, top_count)
    )
    summed_x, summed_p = (
        lax.psum_scatter(token_x, "local", scatter_dimension=0, tiled=True),
        lax.psum_scatter(token_p, "local", scatter_dimension=0, tiled=True),
    )
    return (
        summed_x.astype(jnp.bfloat16),
        summed_p,
        gate_grad[None],
        up_grad[None],
        down_grad[None],
    )


LANES = 128
PIECE = 16
DENSE_TOKENS = 64


def one_hot_rows(source, width):
    columns = lax.broadcasted_iota(jnp.int32, (source.shape[0], width), 1)
    return jnp.where(columns == source, 1.0, 0.0).astype(jnp.bfloat16)


def exchange_kernel(
    node_count,
    local_count,
    tok_hbm,
    grad_hbm,
    ids_hbm,
    slots_hbm,
    probs_hbm,
    gate_hbm,
    up_hbm,
    down_hbm,
    x_ref,
    d_ref,
    dgate_ref,
    dup_ref,
    scaled_ref,
    tail_ref,
    tok_ref,
    grad_ref,
    ids_ref,
    slots_ref,
    probs_ref,
    gate_w,
    up_w,
    down_w,
    pieces,
    probs_node,
    order,
    total,
    out_local,
    in_local,
    out_node,
    in_node,
    small_sem,
    weight_sem,
    send_sem,
    piece_sem,
    prob_send_sem,
    prob_recv_sem,
    local_send_sem,
    local_recv_sem,
    node_send_sem,
    node_recv_sem,
):
    f32, bf16 = jnp.float32, jnp.bfloat16
    node, place = lax.axis_index("node"), lax.axis_index("local")
    experts = node_count * EXP_NODE
    expert = node * local_count + place
    own, width = tok_ref.shape
    tokens = node_count * local_count * own
    hidden_units = gate_w.shape[0]
    chunks = weight_sem.shape[1]
    chunk = hidden_units // chunks
    halves = out_local.shape[0]
    piece_width = width // halves
    quarters = PIECE // (2 * own)
    span = width // quarters
    eighths = PIECE // own
    fine = piece_width // eighths

    small = []
    for index, (source, target) in enumerate(
        (
            (tok_hbm, tok_ref),
            (grad_hbm, grad_ref),
            (ids_hbm, ids_ref),
            (slots_hbm, slots_ref),
            (probs_hbm, probs_ref),
        )
    ):
        copy = pltpu.make_async_copy(source, target, small_sem.at[index])
        copy.start()
        small.append(copy)
    loads = []
    for c in range(chunks):
        for w, (source, target) in enumerate(
            ((gate_hbm, gate_w), (up_hbm, up_w), (down_hbm, down_w))
        ):
            copy = pltpu.make_async_copy(
                source.at[0, pl.ds(c * chunk, chunk), :], target.at[pl.ds(c * chunk, chunk), :], weight_sem.at[w, c]
            )
            copy.start()
            loads.append(copy)

    barrier = pltpu.get_barrier_semaphore()
    for step in range(1, node_count):
        pl.semaphore_signal(
            barrier,
            inc=1,
            device_id=(lax.rem(node + step, node_count), place),
            device_id_type=MESH,
        )
    for step in range(1, local_count):
        pl.semaphore_signal(
            barrier,
            inc=1,
            device_id=(node, lax.rem(place + step, local_count)),
            device_id_type=MESH,
        )

    for copy in small:
        copy.wait()
    kept_ids = jnp.where(slots_ref[...] < CAPN, ids_ref[...], -1)
    probs = probs_ref[...].astype(f32)
    node_tokens, top = kept_ids.shape
    lane = lax.broadcasted_iota(jnp.int32, (node_tokens, LANES), 1)
    dense = jnp.zeros((node_tokens, LANES), f32)
    for k in range(top):
        dense = dense + jnp.where(lane == kept_ids[:, k : k + 1], probs[:, k : k + 1], 0.0)
    row = lax.broadcasted_iota(jnp.int32, (PIECE, span), 0)
    packed = jnp.zeros((PIECE, span), f32)
    for which, source in enumerate((tok_ref, grad_ref)):
        rows = source[...].astype(f32)
        for t in range(own):
            for q in range(quarters):
                packed = jnp.where(
                    row == (which * own + t) * quarters + q,
                    rows[t : t + 1, q * span : (q + 1) * span],
                    packed,
                )
    me = node * local_count + place
    pieces[me] = packed.astype(bf16)
    probs_node[node] = jnp.concatenate(
        [dense, jnp.zeros((PIECE - node_tokens, LANES), f32)], axis=0
    ).astype(bf16)

    pl.semaphore_wait(barrier, node_count + local_count - 2)

    sent = []

    def send_piece(piece, target):
        copy = pltpu.make_async_remote_copy(
            src_ref=pieces.at[piece],
            dst_ref=pieces.at[piece],
            send_sem=send_sem.at[len(sent)],
            recv_sem=piece_sem.at[piece],
            device_id=target,
            device_id_type=MESH,
        )
        copy.start()
        sent.append(copy)

    def await_piece(piece):
        pltpu.make_async_remote_copy(
            src_ref=pieces.at[piece],
            dst_ref=pieces.at[piece],
            send_sem=send_sem.at[0],
            recv_sem=piece_sem.at[piece],
            device_id=(node, place),
            device_id_type=MESH,
        ).wait_recv()

    chips = local_count // 2
    chip, core = place // 2, lax.rem(place, 2)
    mate = (node, chip * 2 + 1 - core)
    for step in range(1, node_count):
        send_piece(me, (lax.rem(node + step, node_count), place))
    for step in range(1, chips):
        send_piece(me, (node, lax.rem(chip + step, chips) * 2 + core))
    send_piece(me, mate)
    copies = []
    for step in range(1, node_count):
        copy = pltpu.make_async_remote_copy(
            src_ref=probs_node.at[node],
            dst_ref=probs_node.at[node],
            send_sem=prob_send_sem.at[step],
            recv_sem=prob_recv_sem.at[node],
            device_id=(lax.rem(node + step, node_count), place),
            device_id_type=MESH,
        )
        copy.start()
        copies.append(copy)

    i = lax.broadcasted_iota(jnp.int32, (order.shape[0], LANES), 0)
    which, q, tok = i // (quarters * tokens), (i // tokens) % quarters, i % tokens
    l, n, t = tok // (own * node_count), (tok // own) % node_count, tok % own
    source = (n * local_count + l) * PIECE + (which * own + t) * quarters + q
    for block in range(order.shape[1] // LANES):
        columns = lax.broadcasted_iota(jnp.int32, (order.shape[0], LANES), 1) + block * LANES
        order[:, block * LANES : (block + 1) * LANES] = jnp.where(
            columns == source, 1.0, 0.0
        ).astype(bf16)

    token_row = lax.broadcasted_iota(jnp.int32, (node_tokens, top), 0)
    eye = lax.broadcasted_iota(jnp.int32, (top, top), 0) == lax.broadcasted_iota(
        jnp.int32, (top, top), 1
    )
    lane = lax.broadcasted_iota(jnp.int32, (top, LANES), 1).astype(f32)
    ids_f = kept_ids.astype(f32)
    for t in range(own):
        ids_row = jnp.sum(
            jnp.where(token_row == place * own + t, ids_f, 0.0), axis=0, keepdims=True
        )
        ids_col = jnp.sum(jnp.where(eye, ids_row, 0.0), axis=1, keepdims=True)
        hit = (ids_col >= 0.0) & ((lane == ids_col) | (lane == ids_col + experts))
        tail_ref[halves + 1, t * top : (t + 1) * top, :] = jnp.where(hit, 1.0, 0.0)
    i = lax.broadcasted_iota(jnp.int32, (tokens, 1), 0)
    l, n, t = i // (own * node_count), (i // own) % node_count, i % own
    prob_order = one_hot_rows(n * PIECE + l * own + t, node_count * PIECE)

    for step in range(1, node_count):
        piece = lax.rem(node + node_count - step, node_count) * local_count + place
        await_piece(piece)
        for hop in range(1, chips):
            send_piece(piece, (node, lax.rem(chip + hop, chips) * 2 + core))
        send_piece(piece, mate)
    for step in range(node_count):
        for hop in range(1, chips):
            piece = (
                lax.rem(node + node_count - step, node_count) * local_count
                + lax.rem(chip + chips - hop, chips) * 2
                + core
            )
            await_piece(piece)
            send_piece(piece, mate)
    for step in range(node_count):
        for hop in range(chips):
            piece = (
                lax.rem(node + node_count - step, node_count) * local_count
                + lax.rem(chip + chips - hop, chips) * 2
                + 1
                - core
            )
            await_piece(piece)

    gathered = pieces[...].reshape(order.shape[0], span)
    for half in range(2):
        columns = span // 2
        at = half * columns
        sorted_rows = jnp.dot(
            order[...], gathered[:, at : at + columns], preferred_element_type=f32
        ).astype(bf16)
        for which, target in enumerate((x_ref, d_ref)):
            for q in range(quarters):
                first = (which * quarters + q) * tokens
                target[:, q * span + at : q * span + at + columns] = sorted_rows[
                    first : first + tokens
                ]
    for step in range(1, node_count):
        peer = lax.rem(node + node_count - step, node_count)
        pltpu.make_async_remote_copy(
            src_ref=probs_node.at[peer],
            dst_ref=probs_node.at[peer],
            send_sem=prob_send_sem.at[0],
            recv_sem=prob_recv_sem.at[peer],
            device_id=(peer, place),
            device_id_type=MESH,
        ).wait_recv()
    weights = jnp.dot(
        prob_order,
        probs_node[...].reshape(node_count * PIECE, LANES),
        preferred_element_type=f32,
    )
    lane = lax.broadcasted_iota(jnp.int32, (tokens, LANES), 1)
    p_col = jnp.sum(jnp.where(lane == expert, weights, 0.0), axis=1, keepdims=True)

    contract_last = (((1,), (1,)), ((), ()))
    pair = jnp.zeros((tokens, 1), f32)
    for c in range(chunks):
        for copy in loads[3 * c : 3 * c + 3]:
            copy.wait()
        at = pl.ds(c * chunk, chunk)
        gate_pre = lax.dot_general(
            x_ref[...], gate_w[at, :], contract_last, preferred_element_type=f32
        )
        up_pre = lax.dot_general(x_ref[...], up_w[at, :], contract_last, preferred_element_type=f32)
        back = lax.dot_general(d_ref[...], down_w[at, :], contract_last, preferred_element_type=f32)
        s = jax.nn.sigmoid(gate_pre)
        activated = gate_pre * s
        hidden = activated * up_pre
        pair = pair + jnp.sum(hidden * back, axis=1, keepdims=True)
        d_hidden = p_col * back
        d_gate = (d_hidden * up_pre * s * (1.0 + gate_pre * (1.0 - s))).astype(bf16)
        d_up = (d_hidden * activated).astype(bf16)
        dgate_ref[:, at] = d_gate
        dup_ref[:, at] = d_up
        scaled_ref[:, at] = (p_col * hidden).astype(bf16)

    high = pair.astype(bf16).astype(f32)
    total[0, :, piece_width:] = jnp.where(
        lane == expert, high, jnp.where(lane == expert + experts, pair - high, 0.0)
    )
    group = own * node_count
    used = [piece_width + (LANES if half == 0 else 0) for half in range(halves)]
    block = piece_width // 2
    out_local[0, :, :, piece_width:] = (
        total[0, :, piece_width:].astype(bf16).reshape(local_count, group, LANES)
    )
    for half in range(halves):
        for at in range(0, piece_width, block):
            columns = pl.ds(half * piece_width + at, block)
            part = jnp.dot(
                dgate_ref[...], gate_w[:, columns], preferred_element_type=f32
            ) + jnp.dot(dup_ref[...], up_w[:, columns], preferred_element_type=f32)
            total[half, :, at : at + block] = part
            out_local[half, :, :, at : at + block] = part.astype(bf16).reshape(
                local_count, group, block
            )
        for step in range(1, local_count):
            peer = lax.rem(place + step, local_count)
            copy = pltpu.make_async_remote_copy(
                src_ref=out_local.at[half, peer, :, pl.ds(0, used[half])],
                dst_ref=in_local.at[half, place, :, pl.ds(0, used[half])],
                send_sem=local_send_sem.at[half, step],
                recv_sem=local_recv_sem.at[half, place],
                device_id=(node, peer),
                device_id_type=MESH,
            )
            copy.start()
            copies.append(copy)

    count = eighths * group
    i = lax.broadcasted_iota(jnp.int32, (count, 1), 0)
    n, t, e = i // PIECE, (i // eighths) % own, i % eighths
    spread = one_hot_rows(e * group + n * own + t, count)
    spread_tail = one_hot_rows(jnp.where(e == 0, n * own + t, -1), group)
    used_node = [fine + (LANES if half == 0 else 0) for half in range(halves)]
    for half in range(halves):
        summed = total[
            half, pl.ds(pl.multiple_of(place * group, group), group), : used[half]
        ]
        for step in range(1, local_count):
            peer = lax.rem(place + local_count - step, local_count)
            pltpu.make_async_remote_copy(
                src_ref=out_local.at[half, peer, :, pl.ds(0, used[half])],
                dst_ref=in_local.at[half, peer, :, pl.ds(0, used[half])],
                send_sem=local_send_sem.at[half, 0],
                recv_sem=local_recv_sem.at[half, peer],
                device_id=(node, peer),
                device_id_type=MESH,
            ).wait_recv()
            summed = summed + in_local[half, peer, :, : used[half]].astype(f32)
        summed = summed.astype(bf16)
        stacked = jnp.concatenate(
            [summed[:, e * fine : (e + 1) * fine] for e in range(eighths)], axis=0
        )
        out_node[half, :, :, :fine] = (
            jnp.dot(spread, stacked, preferred_element_type=f32)
            .astype(bf16)
            .reshape(node_count, PIECE, fine)
        )
        if half == 0:
            out_node[half, :, :, fine:] = (
                jnp.dot(spread_tail, summed[:, piece_width:], preferred_element_type=f32)
                .astype(bf16)
                .reshape(node_count, PIECE, LANES)
            )
        for step in range(1, node_count):
            peer = lax.rem(node + step, node_count)
            copy = pltpu.make_async_remote_copy(
                src_ref=out_node.at[half, peer, :, pl.ds(0, used_node[half])],
                dst_ref=in_node.at[half, node, :, pl.ds(0, used_node[half])],
                send_sem=node_send_sem.at[half, step],
                recv_sem=node_recv_sem.at[half, node],
                device_id=(peer, place),
                device_id_type=MESH,
            )
            copy.start()
            copies.append(copy)
    for half in range(halves):
        result = out_node[half, node, :, : used_node[half]].astype(f32)
        for step in range(1, node_count):
            peer = lax.rem(node + node_count - step, node_count)
            pltpu.make_async_remote_copy(
                src_ref=out_node.at[half, peer, :, pl.ds(0, used_node[half])],
                dst_ref=in_node.at[half, peer, :, pl.ds(0, used_node[half])],
                send_sem=node_send_sem.at[half, 0],
                recv_sem=node_recv_sem.at[half, peer],
                device_id=(peer, place),
                device_id_type=MESH,
            ).wait_recv()
            result = result + in_node[half, peer, :, : used_node[half]].astype(f32)
        tail_ref[half, :, :] = result[:, :fine]
        if half == 0:
            tail_ref[halves, :, :] = result[:, fine:]

    for copy in sent:
        copy.wait_send()
    for copy in copies:
        copy.wait_send()


def outer_kernel(
    x_ref,
    d_ref,
    dgate_ref,
    dup_ref,
    scaled_ref,
    tail_ref,
    gx_ref,
    gp_ref,
    gate_hbm,
    up_hbm,
    down_hbm,
    blocks,
    block_sem,
):
    contract_first = (((0,), (0,)), ((), ()))
    steps, block = blocks.shape[1], blocks.shape[2]
    work = ((dgate_ref, x_ref, gate_hbm), (dup_ref, x_ref, up_hbm), (scaled_ref, d_ref, down_hbm))

    def copy_of(w, step):
        rows = pl.ds(pl.multiple_of(step * block, block), block)
        return pltpu.make_async_copy(
            blocks.at[w, step], work[w][2].at[0, rows, :], block_sem.at[w, step]
        )

    for step in range(steps):
        for w, (left, right, target) in enumerate(work):
            blocks[w, step] = lax.dot_general(
                left[:, step * block : (step + 1) * block],
                right[...],
                contract_first,
                preferred_element_type=jnp.float32,
            )
            copy_of(w, step).start()

    halves = tail_ref.shape[0] - 2
    own, top = gp_ref.shape
    eighths, fine = PIECE // own, tail_ref.shape[2]
    for t in range(own):
        gx_ref[t : t + 1, :] = jnp.concatenate(
            [
                tail_ref[half, t * eighths + e : t * eighths + e + 1, :]
                for half in range(halves)
                for e in range(eighths)
            ],
            axis=1,
        ).astype(jnp.bfloat16)
    eye = lax.broadcasted_iota(jnp.int32, (top, top), 0) == lax.broadcasted_iota(
        jnp.int32, (top, top), 1
    )
    for t in range(own):
        line = tail_ref[halves, t * eighths : t * eighths + 1, :]
        hit = tail_ref[halves + 1, t * top : (t + 1) * top, :]
        found = jnp.sum(jnp.where(hit > 0.5, line, 0.0), axis=1, keepdims=True)
        gp_ref[t : t + 1, :] = jnp.sum(jnp.where(eye, found, 0.0), axis=0, keepdims=True)

    for step in range(steps):
        for w in range(3):
            copy_of(w, step).wait()


def dense_local(
    tok_x, grad_out, expert_ids, slot_ids, route_probs, gate_weight, up_weight, down_weight
):
    node_count, local_count = lax.axis_size("node"), lax.axis_size("local")
    own, width = tok_x.shape
    top = expert_ids.shape[1]
    hidden = gate_weight.shape[1]
    devices = node_count * local_count
    tokens = devices * own
    chunk = 256 if hidden % 256 == 0 else hidden
    chunks = hidden // chunk
    quarters = PIECE // (2 * own)
    span = width // quarters
    halves = 2
    fine = width * own // (PIECE * halves)
    f32, bf16 = jnp.float32, jnp.bfloat16
    vmem = pl.BlockSpec(memory_space=pltpu.VMEM)
    hbm = pl.BlockSpec(memory_space=pltpu.HBM)
    dma = pltpu.SemaphoreType.DMA
    group = own * node_count
    rows_x, rows_d, d_gate, d_up, scaled, tail = pl.pallas_call(
        functools.partial(exchange_kernel, node_count, local_count),
        out_shape=(
            jax.ShapeDtypeStruct((tokens, width), bf16),
            jax.ShapeDtypeStruct((tokens, width), bf16),
            jax.ShapeDtypeStruct((tokens, hidden), bf16),
            jax.ShapeDtypeStruct((tokens, hidden), bf16),
            jax.ShapeDtypeStruct((tokens, hidden), bf16),
            jax.ShapeDtypeStruct((halves + 2, PIECE, fine), f32),
        ),
        in_specs=[hbm] * 8,
        out_specs=(vmem,) * 6,
        scratch_shapes=[
            pltpu.VMEM(tok_x.shape, bf16),
            pltpu.VMEM(grad_out.shape, bf16),
            pltpu.VMEM(expert_ids.shape, expert_ids.dtype),
            pltpu.VMEM(slot_ids.shape, slot_ids.dtype),
            pltpu.VMEM(route_probs.shape, bf16),
            pltpu.VMEM((hidden, width), bf16),
            pltpu.VMEM((hidden, width), bf16),
            pltpu.VMEM((hidden, width), bf16),
            pltpu.VMEM((devices, PIECE, span), bf16),
            pltpu.VMEM((node_count, PIECE, LANES), bf16),
            pltpu.VMEM((devices * PIECE, devices * PIECE), bf16),
            pltpu.VMEM((halves, tokens, width // halves + LANES), f32),
            pltpu.VMEM((halves, local_count, group, width // halves + LANES), bf16),
            pltpu.VMEM((halves, local_count, group, width // halves + LANES), bf16),
            pltpu.VMEM((halves, node_count, PIECE, fine + LANES), bf16),
            pltpu.VMEM((halves, node_count, PIECE, fine + LANES), bf16),
            dma((5,)),
            dma((3, chunks)),
            dma((devices,)),
            dma((devices,)),
            dma((node_count,)),
            dma((node_count,)),
            dma((halves, local_count)),
            dma((halves, local_count)),
            dma((halves, node_count)),
            dma((halves, node_count)),
        ],
        compiler_params=pltpu.CompilerParams(
            collective_id=0, has_side_effects=True, vmem_limit_bytes=48 * 1024 * 1024
        ),
    )(tok_x, grad_out, expert_ids, slot_ids, route_probs, gate_weight, up_weight, down_weight)
    block = 128 if hidden % 128 == 0 else hidden
    grad = jax.ShapeDtypeStruct((1, hidden, width), f32)
    steps = hidden // block
    grad_x, grad_probs, gate_grad, up_grad, down_grad = pl.pallas_call(
        outer_kernel,
        out_shape=(
            jax.ShapeDtypeStruct((own, width), bf16),
            jax.ShapeDtypeStruct((own, top), f32),
            grad,
            grad,
            grad,
        ),
        in_specs=[vmem] * 6,
        out_specs=(vmem, vmem, hbm, hbm, hbm),
        scratch_shapes=[pltpu.VMEM((3, steps, block, width), f32), dma((3, steps))],
        compiler_params=pltpu.CompilerParams(vmem_limit_bytes=40 * 1024 * 1024),
    )(rows_x, rows_d, d_gate, d_up, scaled, tail)
    return grad_x, grad_probs, gate_grad, up_grad, down_grad


def solution(mesh):
    in_specs = (
        P(("node", "local"), None),
        P(("node", "local"), None),
        P("node", None),
        P("node", None),
        P("node", None),
        P(("node", "local"), None, None),
        P(("node", "local"), None, None),
        P(("node", "local"), None, None),
    )
    out_specs = (
        P(("node", "local"), None),
        P(("node", "local"), None),
        P(("node", "local"), None, None),
        P(("node", "local"), None, None),
        P(("node", "local"), None, None),
    )
    node_count, local_count = mesh.shape["node"], mesh.shape["local"]

    def step(*args):
        tokens = args[0].shape[0] * node_count * local_count
        dense = (
            tokens <= DENSE_TOKENS
            and local_count == EXP_NODE
            and 2 * EXP_NODE * node_count <= LANES
        )
        return (dense_local if dense else local)(*args)

    return jax.shard_map(step, mesh=mesh, in_specs=in_specs, out_specs=out_specs, check_vma=False)
```

```python
import functools

import jax
import jax.numpy as jnp
from jax import lax
from jax.experimental import pallas as pl
from jax.experimental.pallas import tpu as pltpu
from jax.sharding import PartitionSpec as P

EXP_NODE = 4
CAPN = 7
MESH = pl.DeviceIdType.MESH


contract_last = (((1,), (1,)), ((), ()))
contract_first = (((0,), (0,)), ((), ()))


def owner_grads(owner_x, owner_d, owner_p, w_gate_rows, w_up_rows, w_down_rows):
    gate_pre = lax.dot_general(
        owner_x, w_gate_rows, contract_last, preferred_element_type=jnp.float32
    )
    up_pre = lax.dot_general(owner_x, w_up_rows, contract_last, preferred_element_type=jnp.float32)
    sigmoid_gate = jax.nn.sigmoid(gate_pre)
    activated = gate_pre * sigmoid_gate
    hidden = activated * up_pre
    back_proj = lax.dot_general(
        owner_d, w_down_rows, contract_last, preferred_element_type=jnp.float32
    )
    pair_grad = jnp.sum(hidden * back_proj, axis=1)
    d_hidden = owner_p[:, None] * back_proj
    d_gate = (d_hidden * up_pre * sigmoid_gate * (1.0 + gate_pre * (1.0 - sigmoid_gate))).astype(
        jnp.bfloat16
    )
    d_up = (d_hidden * activated).astype(jnp.bfloat16)
    scaled_hidden = (owner_p[:, None] * hidden).astype(jnp.bfloat16)
    input_grad = jnp.dot(d_gate, w_gate_rows, preferred_element_type=jnp.float32) + jnp.dot(
        d_up, w_up_rows, preferred_element_type=jnp.float32
    )
    gate_grad = lax.dot_general(d_gate, owner_x, contract_first, preferred_element_type=jnp.float32)
    up_grad = lax.dot_general(d_up, owner_x, contract_first, preferred_element_type=jnp.float32)
    down_grad = lax.dot_general(
        scaled_hidden, owner_d, contract_first, preferred_element_type=jnp.float32
    )
    return (input_grad, pair_grad, gate_grad, up_grad, down_grad)


def local(tok_x, grad_out, expert_ids, slot_ids, route_probs, gate_weight, up_weight, down_weight):
    node_count = lax.axis_size("node")
    owners = lax.axis_size("local") // EXP_NODE
    place = lax.axis_index("local")
    own_class = place // owners
    node_tokens = expert_ids.shape[0]
    top_count = expert_ids.shape[1]
    model_width = tok_x.shape[1]
    pair_count = node_tokens * top_count
    node_x, node_d = (
        lax.all_gather(tok_x, "local", axis=0, tiled=True),
        lax.all_gather(grad_out, "local", axis=0, tiled=True),
    )
    flat_expert = expert_ids.reshape(-1)
    flat_slot = slot_ids.reshape(-1)
    pair_ids = jnp.arange(pair_count, dtype=jnp.int32)
    is_mine = (flat_expert % EXP_NODE == own_class) & (flat_slot < CAPN)
    target = jnp.where(is_mine, flat_expert // EXP_NODE * CAPN + flat_slot, node_count * CAPN)
    slot_table = (
        jnp.full((node_count * CAPN,), pair_count, jnp.int32).at[target].set(pair_ids, mode="drop")
    )
    token_rows = slot_table // top_count
    outbox_p = jnp.take(route_probs.reshape(-1), slot_table, mode="fill", fill_value=0).reshape(
        node_count, CAPN
    )
    outbox_x = jnp.take(node_x, token_rows, axis=0, mode="fill", fill_value=0).reshape(
        node_count, CAPN, model_width
    )
    outbox_d = jnp.take(node_d, token_rows, axis=0, mode="fill", fill_value=0).reshape(
        node_count, CAPN, model_width
    )
    arrived_x, arrived_d, arrived_p = (
        lax.all_to_all(outbox_x, "node", split_axis=0, concat_axis=0, tiled=True),
        lax.all_to_all(outbox_d, "node", split_axis=0, concat_axis=0, tiled=True),
        lax.all_to_all(outbox_p, "node", split_axis=0, concat_axis=0, tiled=True),
    )
    owner_x = arrived_x.reshape(-1, model_width)
    owner_d = arrived_d.reshape(-1, model_width)
    owner_p = arrived_p.reshape(-1).astype(jnp.float32)
    input_grad, pair_grad, gate_grad, up_grad, down_grad = owner_grads(
        owner_x, owner_d, owner_p, gate_weight[0], up_weight[0], down_weight[0]
    )
    token_hits = (token_rows[None, :] == jnp.arange(node_tokens, dtype=jnp.int32)[:, None]).astype(
        jnp.float32
    )
    back_x, back_p = (
        lax.all_to_all(
            input_grad.reshape(node_count, CAPN, model_width),
            "node",
            split_axis=0,
            concat_axis=0,
            tiled=True,
        ),
        lax.all_to_all(
            pair_grad.reshape(node_count, CAPN), "node", split_axis=0, concat_axis=0, tiled=True
        ),
    )
    token_x = jnp.dot(
        token_hits,
        back_x.reshape(-1, model_width),
        precision=lax.Precision.HIGHEST,
        preferred_element_type=jnp.float32,
    )
    token_p = (
        jnp.zeros((pair_count,), jnp.float32)
        .at[slot_table]
        .add(back_p.reshape(-1), mode="drop")
        .reshape(node_tokens, top_count)
    )
    summed_x, summed_p = (
        lax.psum_scatter(token_x, "local", scatter_dimension=0, tiled=True),
        lax.psum_scatter(token_p, "local", scatter_dimension=0, tiled=True),
    )
    return (
        summed_x.astype(jnp.bfloat16),
        summed_p,
        gate_grad[None],
        up_grad[None],
        down_grad[None],
    )


LANES = 128
PIECE = 16
DENSE_TOKENS = 64
VMEM = 64 * 1024 * 1024


def one_hot_rows(source, width):
    columns = lax.broadcasted_iota(jnp.int32, (source.shape[0], width), 1)
    return jnp.where(columns == source, 1.0, 0.0).astype(jnp.bfloat16)


def exchange_kernel(
    node_count,
    local_count,
    tok_hbm,
    grad_hbm,
    ids_hbm,
    slots_hbm,
    probs_hbm,
    gate_hbm,
    up_hbm,
    down_hbm,
    x_hbm,
    d_hbm,
    dgate_hbm,
    dup_hbm,
    scaled_hbm,
    tail_hbm,
    x_ref,
    d_ref,
    dgate_ref,
    dup_ref,
    scaled_ref,
    tail_ref,
    tok_ref,
    grad_ref,
    ids_ref,
    slots_ref,
    probs_ref,
    gate_w,
    up_w,
    down_w,
    pieces,
    probs_node,
    order,
    total,
    out_local,
    in_local,
    out_node,
    in_node,
    small_sem,
    store_sem,
    weight_sem,
    send_sem,
    piece_sem,
    prob_send_sem,
    prob_recv_sem,
    local_send_sem,
    local_recv_sem,
    node_send_sem,
    node_recv_sem,
):
    f32, bf16 = jnp.float32, jnp.bfloat16
    node, place = lax.axis_index("node"), lax.axis_index("local")
    experts = node_count * EXP_NODE
    expert = node * local_count + place
    own, width = tok_ref.shape
    tokens = node_count * local_count * own
    hidden_units = gate_w.shape[0]
    chunks = weight_sem.shape[1]
    chunk = hidden_units // chunks
    halves = out_local.shape[0]
    piece_width = width // halves
    quarters = PIECE // (2 * own)
    span = width // quarters
    eighths = PIECE // own
    fine = piece_width // eighths

    small = []
    for index, (source, target) in enumerate(
        (
            (tok_hbm, tok_ref),
            (grad_hbm, grad_ref),
            (ids_hbm, ids_ref),
            (slots_hbm, slots_ref),
            (probs_hbm, probs_ref),
        )
    ):
        copy = pltpu.make_async_copy(source, target, small_sem.at[index])
        copy.start()
        small.append(copy)
    loads = []
    for c in range(chunks):
        for w, (source, target) in enumerate(
            ((gate_hbm, gate_w), (up_hbm, up_w), (down_hbm, down_w))
        ):
            copy = pltpu.make_async_copy(
                source.at[0, pl.ds(c * chunk, chunk), :], target.at[pl.ds(c * chunk, chunk), :], weight_sem.at[w, c]
            )
            copy.start()
            loads.append(copy)

    barrier = pltpu.get_barrier_semaphore()
    for step in range(1, node_count):
        pl.semaphore_signal(
            barrier,
            inc=1,
            device_id=(lax.rem(node + step, node_count), place),
            device_id_type=MESH,
        )
    for step in range(1, local_count):
        pl.semaphore_signal(
            barrier,
            inc=1,
            device_id=(node, lax.rem(place + step, local_count)),
            device_id_type=MESH,
        )

    for copy in small:
        copy.wait()
    kept_ids = jnp.where(slots_ref[...] < CAPN, ids_ref[...], -1)
    probs = probs_ref[...].astype(f32)
    node_tokens, top = kept_ids.shape
    lane = lax.broadcasted_iota(jnp.int32, (node_tokens, LANES), 1)
    dense = jnp.zeros((node_tokens, LANES), f32)
    for k in range(top):
        dense = dense + jnp.where(lane == kept_ids[:, k : k + 1], probs[:, k : k + 1], 0.0)
    row = lax.broadcasted_iota(jnp.int32, (PIECE, span), 0)
    packed = jnp.zeros((PIECE, span), f32)
    for which, source in enumerate((tok_ref, grad_ref)):
        rows = source[...].astype(f32)
        for t in range(own):
            for q in range(quarters):
                packed = jnp.where(
                    row == (which * own + t) * quarters + q,
                    rows[t : t + 1, q * span : (q + 1) * span],
                    packed,
                )
    me = node * local_count + place
    pieces[me] = packed.astype(bf16)
    probs_node[node] = jnp.concatenate(
        [dense, jnp.zeros((PIECE - node_tokens, LANES), f32)], axis=0
    ).astype(bf16)

    pl.semaphore_wait(barrier, node_count + local_count - 2)

    sent = []

    def send_piece(piece, target):
        copy = pltpu.make_async_remote_copy(
            src_ref=pieces.at[piece],
            dst_ref=pieces.at[piece],
            send_sem=send_sem.at[len(sent)],
            recv_sem=piece_sem.at[piece],
            device_id=target,
            device_id_type=MESH,
        )
        copy.start()
        sent.append(copy)

    def await_piece(piece):
        pltpu.make_async_remote_copy(
            src_ref=pieces.at[piece],
            dst_ref=pieces.at[piece],
            send_sem=send_sem.at[0],
            recv_sem=piece_sem.at[piece],
            device_id=(node, place),
            device_id_type=MESH,
        ).wait_recv()

    chips = local_count // 2
    chip, core = place // 2, lax.rem(place, 2)
    mate = (node, chip * 2 + 1 - core)
    for step in range(1, node_count):
        send_piece(me, (lax.rem(node + step, node_count), place))
    for step in range(1, chips):
        send_piece(me, (node, lax.rem(chip + step, chips) * 2 + core))
    send_piece(me, mate)
    copies = []
    for step in range(1, node_count):
        copy = pltpu.make_async_remote_copy(
            src_ref=probs_node.at[node],
            dst_ref=probs_node.at[node],
            send_sem=prob_send_sem.at[step],
            recv_sem=prob_recv_sem.at[node],
            device_id=(lax.rem(node + step, node_count), place),
            device_id_type=MESH,
        )
        copy.start()
        copies.append(copy)

    i = lax.broadcasted_iota(jnp.int32, (order.shape[0], LANES), 0)
    which, q, tok = i // (quarters * tokens), (i // tokens) % quarters, i % tokens
    l, n, t = tok // (own * node_count), (tok // own) % node_count, tok % own
    source = (n * local_count + l) * PIECE + (which * own + t) * quarters + q
    for block in range(order.shape[1] // LANES):
        columns = lax.broadcasted_iota(jnp.int32, (order.shape[0], LANES), 1) + block * LANES
        order[:, block * LANES : (block + 1) * LANES] = jnp.where(
            columns == source, 1.0, 0.0
        ).astype(bf16)

    token_row = lax.broadcasted_iota(jnp.int32, (node_tokens, top), 0)
    eye = lax.broadcasted_iota(jnp.int32, (top, top), 0) == lax.broadcasted_iota(
        jnp.int32, (top, top), 1
    )
    lane = lax.broadcasted_iota(jnp.int32, (top, LANES), 1).astype(f32)
    ids_f = kept_ids.astype(f32)
    for t in range(own):
        ids_row = jnp.sum(
            jnp.where(token_row == place * own + t, ids_f, 0.0), axis=0, keepdims=True
        )
        ids_col = jnp.sum(jnp.where(eye, ids_row, 0.0), axis=1, keepdims=True)
        hit = (ids_col >= 0.0) & ((lane == ids_col) | (lane == ids_col + experts))
        tail_ref[halves + 1, t * top : (t + 1) * top, :] = jnp.where(hit, 1.0, 0.0)
    i = lax.broadcasted_iota(jnp.int32, (tokens, 1), 0)
    l, n, t = i // (own * node_count), (i // own) % node_count, i % own
    prob_order = one_hot_rows(n * PIECE + l * own + t, node_count * PIECE)

    for step in range(1, node_count):
        piece = lax.rem(node + node_count - step, node_count) * local_count + place
        await_piece(piece)
        for hop in range(1, chips):
            send_piece(piece, (node, lax.rem(chip + hop, chips) * 2 + core))
        send_piece(piece, mate)
    for step in range(node_count):
        for hop in range(1, chips):
            piece = (
                lax.rem(node + node_count - step, node_count) * local_count
                + lax.rem(chip + chips - hop, chips) * 2
                + core
            )
            await_piece(piece)
            send_piece(piece, mate)
    for step in range(node_count):
        for hop in range(chips):
            piece = (
                lax.rem(node + node_count - step, node_count) * local_count
                + lax.rem(chip + chips - hop, chips) * 2
                + 1
                - core
            )
            await_piece(piece)

    gathered = pieces[...].reshape(order.shape[0], span)
    for half in range(2):
        columns = span // 2
        at = half * columns
        sorted_rows = jnp.dot(
            order[...], gathered[:, at : at + columns], preferred_element_type=f32
        ).astype(bf16)
        for which, target in enumerate((x_ref, d_ref)):
            for q in range(quarters):
                first = (which * quarters + q) * tokens
                target[:, q * span + at : q * span + at + columns] = sorted_rows[
                    first : first + tokens
                ]
    for step in range(1, node_count):
        peer = lax.rem(node + node_count - step, node_count)
        pltpu.make_async_remote_copy(
            src_ref=probs_node.at[peer],
            dst_ref=probs_node.at[peer],
            send_sem=prob_send_sem.at[0],
            recv_sem=prob_recv_sem.at[peer],
            device_id=(peer, place),
            device_id_type=MESH,
        ).wait_recv()
    weights = jnp.dot(
        prob_order,
        probs_node[...].reshape(node_count * PIECE, LANES),
        preferred_element_type=f32,
    )
    lane = lax.broadcasted_iota(jnp.int32, (tokens, LANES), 1)
    p_col = jnp.sum(jnp.where(lane == expert, weights, 0.0), axis=1, keepdims=True)

    stores = []

    def store(source, target):
        copy = pltpu.make_async_copy(source, target, store_sem.at[len(stores)])
        copy.start()
        stores.append(copy)

    store(x_ref, x_hbm)
    store(d_ref, d_hbm)
    contract_last = (((1,), (1,)), ((), ()))
    pair = jnp.zeros((tokens, 1), f32)
    for c in range(chunks):
        for copy in loads[3 * c : 3 * c + 3]:
            copy.wait()
        at = pl.ds(c * chunk, chunk)
        gate_pre = lax.dot_general(
            x_ref[...], gate_w[at, :], contract_last, preferred_element_type=f32
        )
        up_pre = lax.dot_general(x_ref[...], up_w[at, :], contract_last, preferred_element_type=f32)
        back = lax.dot_general(d_ref[...], down_w[at, :], contract_last, preferred_element_type=f32)
        s = jax.nn.sigmoid(gate_pre)
        activated = gate_pre * s
        hidden = activated * up_pre
        pair = pair + jnp.sum(hidden * back, axis=1, keepdims=True)
        d_hidden = p_col * back
        d_gate = (d_hidden * up_pre * s * (1.0 + gate_pre * (1.0 - s))).astype(bf16)
        d_up = (d_hidden * activated).astype(bf16)
        dgate_ref[:, at] = d_gate
        dup_ref[:, at] = d_up
        scaled_ref[:, at] = (p_col * hidden).astype(bf16)

    store(dgate_ref, dgate_hbm)
    store(dup_ref, dup_hbm)
    store(scaled_ref, scaled_hbm)
    high = pair.astype(bf16).astype(f32)
    total[0, :, piece_width:] = jnp.where(
        lane == expert, high, jnp.where(lane == expert + experts, pair - high, 0.0)
    )
    group = own * node_count
    used = [piece_width + (LANES if half == 0 else 0) for half in range(halves)]
    block = piece_width // 2
    out_local[0, :, :, piece_width:] = (
        total[0, :, piece_width:].astype(bf16).reshape(local_count, group, LANES)
    )
    for half in range(halves):
        for at in range(0, piece_width, block):
            columns = pl.ds(half * piece_width + at, block)
            part = jnp.dot(
                dgate_ref[...], gate_w[:, columns], preferred_element_type=f32
            ) + jnp.dot(dup_ref[...], up_w[:, columns], preferred_element_type=f32)
            total[half, :, at : at + block] = part
            out_local[half, :, :, at : at + block] = part.astype(bf16).reshape(
                local_count, group, block
            )
        for step in range(1, local_count):
            peer = lax.rem(place + step, local_count)
            copy = pltpu.make_async_remote_copy(
                src_ref=out_local.at[half, peer, :, pl.ds(0, used[half])],
                dst_ref=in_local.at[half, place, :, pl.ds(0, used[half])],
                send_sem=local_send_sem.at[half, step],
                recv_sem=local_recv_sem.at[half, place],
                device_id=(node, peer),
                device_id_type=MESH,
            )
            copy.start()
            copies.append(copy)

    count = eighths * group
    i = lax.broadcasted_iota(jnp.int32, (count, 1), 0)
    n, t, e = i // PIECE, (i // eighths) % own, i % eighths
    spread = one_hot_rows(e * group + n * own + t, count)
    spread_tail = one_hot_rows(jnp.where(e == 0, n * own + t, -1), group)
    used_node = [fine + (LANES if half == 0 else 0) for half in range(halves)]
    for half in range(halves):
        summed = total[
            half, pl.ds(pl.multiple_of(place * group, group), group), : used[half]
        ]
        for step in range(1, local_count):
            peer = lax.rem(place + local_count - step, local_count)
            pltpu.make_async_remote_copy(
                src_ref=out_local.at[half, peer, :, pl.ds(0, used[half])],
                dst_ref=in_local.at[half, peer, :, pl.ds(0, used[half])],
                send_sem=local_send_sem.at[half, 0],
                recv_sem=local_recv_sem.at[half, peer],
                device_id=(node, peer),
                device_id_type=MESH,
            ).wait_recv()
            summed = summed + in_local[half, peer, :, : used[half]].astype(f32)
        summed = summed.astype(bf16)
        stacked = jnp.concatenate(
            [summed[:, e * fine : (e + 1) * fine] for e in range(eighths)], axis=0
        )
        out_node[half, :, :, :fine] = (
            jnp.dot(spread, stacked, preferred_element_type=f32)
            .astype(bf16)
            .reshape(node_count, PIECE, fine)
        )
        if half == 0:
            out_node[half, :, :, fine:] = (
                jnp.dot(spread_tail, summed[:, piece_width:], preferred_element_type=f32)
                .astype(bf16)
                .reshape(node_count, PIECE, LANES)
            )
        for step in range(1, node_count):
            peer = lax.rem(node + step, node_count)
            copy = pltpu.make_async_remote_copy(
                src_ref=out_node.at[half, peer, :, pl.ds(0, used_node[half])],
                dst_ref=in_node.at[half, node, :, pl.ds(0, used_node[half])],
                send_sem=node_send_sem.at[half, step],
                recv_sem=node_recv_sem.at[half, node],
                device_id=(peer, place),
                device_id_type=MESH,
            )
            copy.start()
            copies.append(copy)
    for half in range(halves):
        result = out_node[half, node, :, : used_node[half]].astype(f32)
        for step in range(1, node_count):
            peer = lax.rem(node + node_count - step, node_count)
            pltpu.make_async_remote_copy(
                src_ref=out_node.at[half, peer, :, pl.ds(0, used_node[half])],
                dst_ref=in_node.at[half, peer, :, pl.ds(0, used_node[half])],
                send_sem=node_send_sem.at[half, 0],
                recv_sem=node_recv_sem.at[half, peer],
                device_id=(peer, place),
                device_id_type=MESH,
            ).wait_recv()
            result = result + in_node[half, peer, :, : used_node[half]].astype(f32)
        tail_ref[half, :, :] = result[:, :fine]
        if half == 0:
            tail_ref[halves, :, :] = result[:, fine:]
    store(tail_ref, tail_hbm)

    for copy in sent:
        copy.wait_send()
    for copy in copies:
        copy.wait_send()
    for copy in stores:
        copy.wait()


def outer_kernel(
    x_hbm,
    d_hbm,
    dgate_hbm,
    dup_hbm,
    scaled_hbm,
    tail_hbm,
    gx_ref,
    gp_ref,
    gate_hbm,
    up_hbm,
    down_hbm,
    x_ref,
    d_ref,
    dgate_ref,
    dup_ref,
    scaled_ref,
    tail_ref,
    blocks,
    load_sem,
    block_sem,
):
    contract_first = (((0,), (0,)), ((), ()))
    steps, block, width = blocks.shape[1:]
    loads = []
    for index, (source, target) in enumerate(
        (
            (dgate_hbm, dgate_ref),
            (x_hbm, x_ref),
            (dup_hbm, dup_ref),
            (scaled_hbm, scaled_ref),
            (d_hbm, d_ref),
            (tail_hbm, tail_ref),
        )
    ):
        copy = pltpu.make_async_copy(source, target, load_sem.at[index])
        copy.start()
        loads.append(copy)
    needs = (loads[:2], loads[2:3], loads[3:5])
    tile = 256 if width % 256 == 0 else width
    work = ((dgate_ref, x_ref, gate_hbm), (dup_ref, x_ref, up_hbm), (scaled_ref, d_ref, down_hbm))

    def copy_of(w, step):
        rows = pl.ds(pl.multiple_of(step * block, block), block)
        return pltpu.make_async_copy(
            blocks.at[w, step], work[w][2].at[0, rows, :], block_sem.at[w, step]
        )

    for w, (left, right, target) in enumerate(work):
        for copy in needs[w]:
            copy.wait()
        for step in range(steps):
            for at in range(0, width, tile):
                blocks[w, step, :, at : at + tile] = lax.dot_general(
                    left[:, step * block : (step + 1) * block],
                    right[:, at : at + tile],
                    contract_first,
                    preferred_element_type=jnp.float32,
                )
            copy_of(w, step).start()

    loads[5].wait()
    halves = tail_ref.shape[0] - 2
    own, top = gp_ref.shape
    eighths, fine = PIECE // own, tail_ref.shape[2]
    for t in range(own):
        gx_ref[t : t + 1, :] = jnp.concatenate(
            [
                tail_ref[half, t * eighths + e : t * eighths + e + 1, :]
                for half in range(halves)
                for e in range(eighths)
            ],
            axis=1,
        ).astype(jnp.bfloat16)
    eye = lax.broadcasted_iota(jnp.int32, (top, top), 0) == lax.broadcasted_iota(
        jnp.int32, (top, top), 1
    )
    for t in range(own):
        line = tail_ref[halves, t * eighths : t * eighths + 1, :]
        hit = tail_ref[halves + 1, t * top : (t + 1) * top, :]
        found = jnp.sum(jnp.where(hit > 0.5, line, 0.0), axis=1, keepdims=True)
        gp_ref[t : t + 1, :] = jnp.sum(jnp.where(eye, found, 0.0), axis=0, keepdims=True)

    for step in range(steps):
        for w in range(3):
            copy_of(w, step).wait()


def dense_local(
    tok_x, grad_out, expert_ids, slot_ids, route_probs, gate_weight, up_weight, down_weight
):
    node_count, local_count = lax.axis_size("node"), lax.axis_size("local")
    own, width = tok_x.shape
    top = expert_ids.shape[1]
    hidden = gate_weight.shape[1]
    devices = node_count * local_count
    tokens = devices * own
    chunk = 256 if hidden % 256 == 0 else hidden
    chunks = hidden // chunk
    quarters = PIECE // (2 * own)
    span = width // quarters
    halves = 2
    fine = width * own // (PIECE * halves)
    f32, bf16 = jnp.float32, jnp.bfloat16
    vmem = pl.BlockSpec(memory_space=pltpu.VMEM)
    hbm = pl.BlockSpec(memory_space=pltpu.HBM)
    dma = pltpu.SemaphoreType.DMA
    group = own * node_count
    rows_x, rows_d, d_gate, d_up, scaled, tail = pl.pallas_call(
        functools.partial(exchange_kernel, node_count, local_count),
        out_shape=(
            jax.ShapeDtypeStruct((tokens, width), bf16),
            jax.ShapeDtypeStruct((tokens, width), bf16),
            jax.ShapeDtypeStruct((tokens, hidden), bf16),
            jax.ShapeDtypeStruct((tokens, hidden), bf16),
            jax.ShapeDtypeStruct((tokens, hidden), bf16),
            jax.ShapeDtypeStruct((halves + 2, PIECE, fine), f32),
        ),
        in_specs=[hbm] * 8,
        out_specs=(hbm,) * 6,
        scratch_shapes=[
            pltpu.VMEM((tokens, width), bf16),
            pltpu.VMEM((tokens, width), bf16),
            pltpu.VMEM((tokens, hidden), bf16),
            pltpu.VMEM((tokens, hidden), bf16),
            pltpu.VMEM((tokens, hidden), bf16),
            pltpu.VMEM((halves + 2, PIECE, fine), f32),
            pltpu.VMEM(tok_x.shape, bf16),
            pltpu.VMEM(grad_out.shape, bf16),
            pltpu.VMEM(expert_ids.shape, expert_ids.dtype),
            pltpu.VMEM(slot_ids.shape, slot_ids.dtype),
            pltpu.VMEM(route_probs.shape, bf16),
            pltpu.VMEM((hidden, width), bf16),
            pltpu.VMEM((hidden, width), bf16),
            pltpu.VMEM((hidden, width), bf16),
            pltpu.VMEM((devices, PIECE, span), bf16),
            pltpu.VMEM((node_count, PIECE, LANES), bf16),
            pltpu.VMEM((devices * PIECE, devices * PIECE), bf16),
            pltpu.VMEM((halves, tokens, width // halves + LANES), f32),
            pltpu.VMEM((halves, local_count, group, width // halves + LANES), bf16),
            pltpu.VMEM((halves, local_count, group, width // halves + LANES), bf16),
            pltpu.VMEM((halves, node_count, PIECE, fine + LANES), bf16),
            pltpu.VMEM((halves, node_count, PIECE, fine + LANES), bf16),
            dma((5,)),
            dma((6,)),
            dma((3, chunks)),
            dma((devices,)),
            dma((devices,)),
            dma((node_count,)),
            dma((node_count,)),
            dma((halves, local_count)),
            dma((halves, local_count)),
            dma((halves, node_count)),
            dma((halves, node_count)),
        ],
        compiler_params=pltpu.CompilerParams(
            collective_id=0, has_side_effects=True, vmem_limit_bytes=VMEM
        ),
    )(tok_x, grad_out, expert_ids, slot_ids, route_probs, gate_weight, up_weight, down_weight)
    block = 128 if hidden % 128 == 0 else hidden
    grad = jax.ShapeDtypeStruct((1, hidden, width), f32)
    steps = hidden // block
    grad_x, grad_probs, gate_grad, up_grad, down_grad = pl.pallas_call(
        outer_kernel,
        out_shape=(
            jax.ShapeDtypeStruct((own, width), bf16),
            jax.ShapeDtypeStruct((own, top), f32),
            grad,
            grad,
            grad,
        ),
        in_specs=[hbm] * 6,
        out_specs=(vmem, vmem, hbm, hbm, hbm),
        scratch_shapes=[
            pltpu.VMEM((tokens, width), bf16),
            pltpu.VMEM((tokens, width), bf16),
            pltpu.VMEM((tokens, hidden), bf16),
            pltpu.VMEM((tokens, hidden), bf16),
            pltpu.VMEM((tokens, hidden), bf16),
            pltpu.VMEM((halves + 2, PIECE, fine), f32),
            pltpu.VMEM((3, steps, block, width), f32),
            dma((6,)),
            dma((3, steps)),
        ],
        compiler_params=pltpu.CompilerParams(vmem_limit_bytes=VMEM),
    )(rows_x, rows_d, d_gate, d_up, scaled, tail)
    return grad_x, grad_probs, gate_grad, up_grad, down_grad


def solution(mesh):
    in_specs = (
        P(("node", "local"), None),
        P(("node", "local"), None),
        P("node", None),
        P("node", None),
        P("node", None),
        P(("node", "local"), None, None),
        P(("node", "local"), None, None),
        P(("node", "local"), None, None),
    )
    out_specs = (
        P(("node", "local"), None),
        P(("node", "local"), None),
        P(("node", "local"), None, None),
        P(("node", "local"), None, None),
        P(("node", "local"), None, None),
    )
    node_count, local_count = mesh.shape["node"], mesh.shape["local"]

    def step(*args):
        tokens = args[0].shape[0] * node_count * local_count
        dense = (
            tokens <= DENSE_TOKENS
            and local_count == EXP_NODE
            and 2 * EXP_NODE * node_count <= LANES
        )
        return (dense_local if dense else local)(*args)

    return jax.shard_map(step, mesh=mesh, in_specs=in_specs, out_specs=out_specs, check_vma=False)
```
